32 devices in a mesh: wide: 8 (over z, x), narrow: 4 (over y, core).
Axes of the slice: x: 2, y: 2, z: 4, core: 2. Of those that a mesh axis runs over, the one named last changes fastest.
Arguments:
- tensor_slab: float32 [512, 256, 1024], P(None, 'wide', 'narrow'), may hold values from -220 to 220
- start_basis: float32 [512, 64], replicated, may hold values from -6 to 6
Outputs:
- factor_basis: float32 [512, 64], replicated
- core_unfold: float32 [1024, 64, 256], P('narrow', 'wide')
The draws below stay inside these ranges and needn't reach their ends.
All inputs are finite; a program needn't handle non-finite values.
Results may differ from the reference program's by a relative error of at most 0.0003.
Values sent between devices are 32-bit elements; how exact they have to be, the bound alone decides.
No kernel may reach another device: no remote copies, remote signals or barrier semaphores. Data moves between devices by JAX's collectives and lax.ppermute only.
A program may use at most 64 MiB of HBM per device.

```python
import jax
import jax.numpy as jnp
import numpy as np
from jax import lax

I1 = 512
RANK = 64
ITERS = 8
I2 = 256
I3 = 1024


def hadamard_rows(values):
    row_count = values.shape[0]
    half_width = 1
    while half_width < row_count:
        blocks = values.reshape(row_count // (2 * half_width), 2, half_width, -1)
        upper_half = blocks[:, 0]
        lower_half = blocks[:, 1]
        values = jnp.stack([upper_half + lower_half, upper_half - lower_half], axis=1).reshape(row_count, -1)
        half_width = half_width * 2
    return values


def draw_tensor_slab(key, part):
    key_base = jax.random.fold_in(key, 11)
    key_rows = jax.random.fold_in(key, 12)
    key_fiber = jax.random.fold_in(key, 13)
    key_second = jax.random.fold_in(key, 14)
    decay_rate = 0.993
    first_levels = jax.random.randint(key_base, (I1, I2 * I3), -48, 49)
    second_levels = jax.random.randint(key_second, (I1, I2 * I3), -48, 49)
    levels = (first_levels + second_levels).astype(jnp.float32)
    amplitude = jnp.asarray(np.floor(64.0 * decay_rate ** np.arange(I1) + 0.5), jnp.float32)
    mixed_rows = hadamard_rows(levels * amplitude[:, None]) / 16384.0
    base_field = jnp.clip(mixed_rows, -4.0, 4.0).reshape(I1, I2, I3)
    row_scale = jnp.exp(jax.random.uniform(key_rows, (I1, 1, 1), jnp.float32, -1.2, 1.1))
    fiber_scale = jnp.exp(jax.random.uniform(key_fiber, (1, I2, I3), jnp.float32, -0.69, 0.69))
    ramp_second = 1.0 + 2.0 * jnp.arange(I2, dtype=jnp.float32) / max(I2 - 1, 1)
    ramp_third = 1.0 + 2.0 * jnp.arange(I3, dtype=jnp.float32) / max(I3 - 1, 1)
    return base_field * row_scale * fiber_scale * ramp_second[None, :, None] * ramp_third[None, None, :]


def normal_values(stream_key, dims, scale, bound, kind=jnp.bfloat16):
    entries = scale * jax.random.normal(stream_key, dims, jnp.float32)
    return jnp.clip(entries, min=-bound, max=bound).astype(kind)


def setup_inputs(seed: int = 0) -> dict:
    keys = jax.random.split(jax.random.key(seed), 3)
    return {
        "tensor_slab": draw_tensor_slab(jax.random.fold_in(keys[2], 71), 0),
        "start_basis": normal_values(keys[1], (I1, RANK), 1.0, 6.0, jnp.float32),
    }


def orthonormal(block, inner):
    lower_factor = jnp.linalg.cholesky(inner)
    return jax.scipy.linalg.solve_triangular(lower_factor, block.T, lower=True).T

def reference(tensor_slab, start_basis):
    highest = lax.Precision.HIGHEST
    unfold = tensor_slab.reshape(I1, -1)
    gram = jnp.dot(unfold.astype(jnp.float32), unfold.T.astype(jnp.float32), precision=highest, preferred_element_type=jnp.float32)
    basis = start_basis
    for sweep_index in range(ITERS):
        block = jnp.dot(gram, basis, precision=highest)
        basis = orthonormal(block, jnp.dot(block.T, block, precision=highest))
    core_unfold = jnp.einsum('ir,ijl->lrj', basis, tensor_slab, precision=highest)
    return (basis, core_unfold)
```

```python
import functools

import jax
import jax.numpy as jnp
from jax import lax
from jax.experimental import pallas as pl
from jax.experimental.pallas import tpu as pltpu
from jax.sharding import PartitionSpec as P

ITERS = 8
LANES = 128
ROWS = 8
MIB = 2**20
NT = (((1,), (1,)), ((), ()))
NN = (((1,), (0,)), ((), ()))
f32, bf16 = jnp.float32, jnp.bfloat16


def dot(a, b, dims):
    return lax.dot_general(a, b, dims, preferred_element_type=f32)


def dot_full(a, b, dims):
    return lax.dot_general(a, b, dims, precision=lax.Precision.HIGHEST, preferred_element_type=f32)


def two(x):
    high = x.astype(bf16)
    return high, (x - high.astype(f32)).astype(bf16)


def dot_two(a, b, dims):
    (a_high, a_low), (b_high, b_low) = a, b
    return dot(a_high, b_high, dims) + (dot(a_high, b_low, dims) + dot(a_low, b_high, dims))


def upper_blocks(n):
    return [(p, q) for p in range(n // LANES) for q in range(p, n // LANES)]


def split_rows(x_ref, first, count, high, low):
    rows, depth, lanes = x_ref.shape
    flat = x_ref.reshape(rows * depth, lanes)
    for j in range(count):
        a, b = two(flat[pl.ds(first + j, rows, stride=depth), :])
        high[:, j * lanes : (j + 1) * lanes] = a
        low[:, j * lanes : (j + 1) * lanes] = b


def gram_kernel(x_ref, g_ref, high_0, low_0, high_1, low_1, top, cross, bottom, mixed):
    rows, depth, _ = x_ref.shape
    half = rows // 2
    steps = pl.num_programs(0) * pl.num_programs(1)
    step = pl.program_id(0) * pl.num_programs(1) + pl.program_id(1)

    def add(high, low):
        mixed[...] += dot(high[...], low[...], NT)
        top[...] += dot(high[:half], high[:half], NT)
        cross[...] += dot(high[:half], high[half:], NT)
        bottom[...] += dot(high[half:], high[half:], NT)

    @pl.when(step == 0)
    def _():
        for total in (top, cross, bottom, mixed):
            total[...] = jnp.zeros_like(total)
        split_rows(x_ref, 0, depth // 2, high_0, low_0)
        split_rows(x_ref, depth // 2, depth // 2, high_1, low_1)
        add(high_0, low_0)

    @pl.when(step > 0)
    def _():
        add(high_1, low_1)
        split_rows(x_ref, 0, depth // 2, high_0, low_0)
        add(high_0, low_0)
        split_rows(x_ref, depth // 2, depth // 2, high_1, low_1)

    @pl.when(step == steps - 1)
    def _():
        add(high_1, low_1)
        for k, (p, q) in enumerate(upper_blocks(rows)):
            in_half = half // LANES
            total = top if q < in_half else cross if p < in_half else bottom
            a, b = p % in_half * LANES, q % in_half * LANES
            at_p, at_q = slice(p * LANES, (p + 1) * LANES), slice(q * LANES, (q + 1) * LANES)
            g_ref[k * LANES : (k + 1) * LANES] = (
                total[a : a + LANES, b : b + LANES] + mixed[at_p, at_q] + mixed[at_q, at_p].T
            )


def local_gram(slab):
    rows, second, third = slab.shape
    depth = ROWS
    half = rows // 2
    out = (len(upper_blocks(rows)) * LANES, LANES)
    return pl.pallas_call(
        gram_kernel,
        grid=(second // depth, third // LANES),
        in_specs=[pl.BlockSpec((rows, depth, LANES), lambda j, l: (0, j, l))],
        out_specs=pl.BlockSpec(out, lambda j, l: (0, 0)),
        out_shape=jax.ShapeDtypeStruct(out, f32),
        scratch_shapes=[pltpu.VMEM((rows, depth // 2 * LANES), bf16)] * 4
        + [pltpu.VMEM((half, half), f32)] * 3
        + [pltpu.VMEM((rows, rows), f32)],
        compiler_params=pltpu.CompilerParams(vmem_limit_bytes=32 * MIB),
        name="gram",
    )(slab)


def swap(x, axis, size, bit):
    return lax.ppermute(x, axis, [(i, i ^ bit) for i in range(size)])


def keep_half(x, axis, size, bit):
    halves = x.reshape(2, x.shape[0] // 2, *x.shape[1:])
    mine = (lax.axis_index(axis) & bit) // bit
    keep = lax.dynamic_index_in_dim(halves, mine, 0, keepdims=False)
    send = lax.dynamic_index_in_dim(halves, 1 - mine, 0, keepdims=False)
    return keep + swap(send, axis, size, bit)


def join_half(x, axis, size, bit):
    other = swap(x, axis, size, bit)
    mine = (lax.axis_index(axis) & bit) // bit
    return jnp.where(mine == 0, jnp.concatenate([x, other]), jnp.concatenate([other, x]))


def total(x, wide, narrow):
    halving = [("narrow", narrow, 1 << k) for k in range(narrow.bit_length() - 1)] + [("wide", wide, 1)]
    for axis, size, bit in halving:
        x = keep_half(x, axis, size, bit)
    bits = range(2, wide, 2)
    others = {bit: swap(x, "wide", wide, bit) for bit in bits}
    terms = [x] + [others[bit] for bit in bits]
    while len(terms) > 1:
        terms = [terms[i] + terms[i + 1] for i in range(0, len(terms), 2)]
    x = terms[0]
    for axis, size, bit in reversed(halving):
        x = join_half(x, axis, size, bit)
    return x


def row_of(v, j):
    return jnp.broadcast_to(v[j : j + 1, :], v.shape)


def column_of(v, j):
    return jnp.broadcast_to(v[:, j : j + 1], v.shape)


def inverse_factor(inner, exact):
    n = inner.shape[0]
    groups = n // ROWS
    row = lax.broadcasted_iota(jnp.int32, (ROWS, 2 * n), 0)
    unit = lax.broadcasted_iota(jnp.int32, (n, n), 0) == lax.broadcasted_iota(jnp.int32, (n, n), 1)
    both = jnp.concatenate([inner, unit.astype(f32)], axis=1)
    m = [both[ROWS * q : ROWS * (q + 1)] for q in range(groups)]
    out = []
    for p in range(groups):
        column = {(q, j): column_of(m[q], ROWS * p + j) for q in range(p, groups) for j in range(ROWS)}
        pivots = None
        for j in range(ROWS):
            pivot = row_of(column[p, j], j)
            inverse = pltpu.reciprocal(pivot, approx=True)
            if exact:
                inverse = inverse * (2.0 - pivot * inverse)
                inverse = inverse * (2.0 - pivot * inverse)
            pivots = pivot if pivots is None else jnp.where(row >= j, pivot, pivots)
            later = {k: row_of(column[p, k], j) for k in range(j + 1, ROWS)}
            pivot_row = row_of(m[p], j)
            for q in range(p, groups):
                factor = column[q, j] * inverse
                if q == p:
                    factor = jnp.where(row > j, factor, 0.0)
                for k in range(j + 1, ROWS):
                    column[q, k] = column[q, k] - factor * later[k]
                m[q] = m[q] - factor * pivot_row
        scale = lax.rsqrt(pivots)
        if exact:
            scale = scale * (1.5 - 0.5 * pivots * scale * scale)
        out.append(m[p] * scale)
    return jnp.concatenate(out, axis=0)[:, n:]


def iterate_kernel(packed_ref, start_ref, basis_ref, high, low):
    for k, (p, q) in enumerate(upper_blocks(high.shape[0])):
        at_p, at_q = slice(p * LANES, (p + 1) * LANES), slice(q * LANES, (q + 1) * LANES)
        block = packed_ref[k * LANES : (k + 1) * LANES]
        high[at_p, at_q], low[at_p, at_q] = two(block)
        if p != q:
            high[at_q, at_p], low[at_q, at_p] = two(block.T)

    def times_gram(b):
        return dot_two(b, (high[...], low[...]), NN)

    basis_ref[...] = times_gram(two(start_ref[...]))

    def sweep(_, carry):
        block = two(basis_ref[...])
        product = times_gram(block)
        inverse = inverse_factor(dot_two(block, block, NT), False)
        basis_ref[...] = dot_two(two(inverse), two(product), NN)
        return carry

    lax.fori_loop(0, ITERS - 1, sweep, 0)
    block = basis_ref[...]
    inverse = inverse_factor(dot_full(block, block, NT), True)
    basis_ref[...] = dot_full(inverse, block, NN)


def iterate(packed, start):
    rank, n = start.shape
    return pl.pallas_call(
        iterate_kernel,
        in_specs=[pl.BlockSpec(memory_space=pltpu.VMEM)] * 2,
        out_specs=pl.BlockSpec(memory_space=pltpu.VMEM),
        out_shape=jax.ShapeDtypeStruct((rank, n), f32),
        scratch_shapes=[pltpu.VMEM((n, n), bf16)] * 2,
        compiler_params=pltpu.CompilerParams(vmem_limit_bytes=32 * MIB),
        name="iterate",
    )(packed, start)


def core_kernel(basis_ref, x_ref, out_ref):
    rows, depth, lanes = x_ref.shape
    rank = basis_ref.shape[0]
    groups = out_ref.shape[0]
    flat = x_ref.reshape(rows * depth, lanes)
    basis = jnp.concatenate(two(basis_ref[...]), axis=0)
    for j in range(0, depth, 2):
        pair = [two(flat[pl.ds(j + k, rows, stride=depth), :]) for k in range(2)]
        high, low = (jnp.concatenate(half, axis=1) for half in zip(*pair))
        by_high = dot(basis, high, NN)
        total = by_high[:rank] + (by_high[rank:] + dot(basis[:rank], low, NN))
        for k in range(2):
            piece = total[:, k * lanes : (k + 1) * lanes]
            for g in range(groups):
                size = rank // groups
                out_ref[g, 0, j + k] = piece[g * size : (g + 1) * size]


def truncate(basis, slab, groups):
    rows, second, third = slab.shape
    rank = basis.shape[0]
    depth = ROWS
    return pl.pallas_call(
        core_kernel,
        grid=(second // depth, third // LANES),
        in_specs=[
            pl.BlockSpec((rank, rows), lambda j, l: (0, 0)),
            pl.BlockSpec((rows, depth, LANES), lambda j, l: (0, j, l)),
        ],
        out_specs=pl.BlockSpec((groups, 1, depth, rank // groups, LANES), lambda j, l: (0, l, j, 0, 0)),
        out_shape=jax.ShapeDtypeStruct((groups, third // LANES, second, rank // groups, LANES), f32),
        compiler_params=pltpu.CompilerParams(vmem_limit_bytes=32 * MIB),
        name="truncate",
    )(basis, slab)


def turn_kernel(in_ref, out_ref):
    sources, _, second, rank, lanes = in_ref.shape
    flat = in_ref.reshape(sources * second * rank, lanes)
    flat_out = out_ref.reshape(lanes * rank, LANES)
    for r in range(rank):
        flat_out[pl.ds(r, lanes, stride=rank), :] = flat[pl.ds(r, sources * second, stride=rank), :].T


def turn(parts):
    sources, blocks, second, rank, lanes = parts.shape
    step = LANES // second
    return pl.pallas_call(
        turn_kernel,
        grid=(blocks, sources // step),
        in_specs=[pl.BlockSpec((step, 1, second, rank, lanes), lambda l, s: (s, l, 0, 0, 0))],
        out_specs=pl.BlockSpec((lanes, rank, LANES), lambda l, s: (l, 0, s)),
        out_shape=jax.ShapeDtypeStruct((blocks * lanes, rank, sources * second), f32),
        compiler_params=pltpu.CompilerParams(vmem_limit_bytes=32 * MIB),
        name="turn",
    )(parts)


def shards(wide, narrow, tensor_slab, start_basis):
    packed = total(local_gram(tensor_slab), wide, narrow)
    basis = iterate(packed, start_basis.T)
    parts = truncate(basis, tensor_slab, wide)
    parts = lax.all_to_all(parts, "wide", split_axis=0, concat_axis=0, tiled=True)
    return basis.T, turn(parts)


def solution(mesh):
    return jax.shard_map(
        functools.partial(shards, mesh.shape["wide"], mesh.shape["narrow"]),
        mesh=mesh,
        in_specs=(P(None, "wide", "narrow"), P()),
        out_specs=(P(), P("narrow", "wide", None)),
        check_vma=False,
    )
```

```python
import functools

import jax
import jax.numpy as jnp
from jax import lax
from jax.experimental import pallas as pl
from jax.experimental.pallas import tpu as pltpu
from jax.sharding import PartitionSpec as P

ITERS = 8
LANES = 128
ROWS = 8
DEPTH = 4
MIB = 2**20
NT = (((1,), (1,)), ((), ()))
NN = (((1,), (0,)), ((), ()))
f32, bf16 = jnp.float32, jnp.bfloat16


def dot(a, b, dims):
    return lax.dot_general(a, b, dims, preferred_element_type=f32)


def dot_full(a, b, dims):
    return lax.dot_general(a, b, dims, precision=lax.Precision.HIGHEST, preferred_element_type=f32)


def two(x):
    high = x.astype(bf16)
    return high, (x - high.astype(f32)).astype(bf16)


def dot_two(a, b, dims):
    (a_high, a_low), (b_high, b_low) = a, b
    return dot(a_high, b_high, dims) + (dot(a_high, b_low, dims) + dot(a_low, b_high, dims))


def upper_blocks(n):
    return [(p, q) for p in range(n // LANES) for q in range(p, n // LANES)]


def split_rows(x_ref, first, count, high, low):
    rows, depth, lanes = x_ref.shape
    flat = x_ref.reshape(rows * depth, lanes)
    for j in range(count):
        a, b = two(flat[pl.ds(first + j, rows, stride=depth), :])
        high[:, j * lanes : (j + 1) * lanes] = a
        low[:, j * lanes : (j + 1) * lanes] = b


def gram_kernel(x_ref, g_ref, high_0, low_0, high_1, low_1, top, cross, bottom, mixed):
    rows, depth, _ = x_ref.shape
    half = rows // 2
    steps = pl.num_programs(0) * pl.num_programs(1)
    step = pl.program_id(0) * pl.num_programs(1) + pl.program_id(1)

    def add(high, low):
        mixed[...] += dot(high[...], low[...], NT)
        top[...] += dot(high[:half], high[:half], NT)
        cross[...] += dot(high[:half], high[half:], NT)
        bottom[...] += dot(high[half:], high[half:], NT)

    @pl.when(step == 0)
    def _():
        for total in (top, cross, bottom, mixed):
            total[...] = jnp.zeros_like(total)
        split_rows(x_ref, 0, depth // 2, high_0, low_0)
        split_rows(x_ref, depth // 2, depth // 2, high_1, low_1)
        add(high_0, low_0)

    @pl.when(step > 0)
    def _():
        add(high_1, low_1)
        split_rows(x_ref, 0, depth // 2, high_0, low_0)
        add(high_0, low_0)
        split_rows(x_ref, depth // 2, depth // 2, high_1, low_1)

    @pl.when(step == steps - 1)
    def _():
        add(high_1, low_1)
        for k, (p, q) in enumerate(upper_blocks(rows)):
            in_half = half // LANES
            total = top if q < in_half else cross if p < in_half else bottom
            a, b = p % in_half * LANES, q % in_half * LANES
            at_p, at_q = slice(p * LANES, (p + 1) * LANES), slice(q * LANES, (q + 1) * LANES)
            g_ref[k * LANES : (k + 1) * LANES] = (
                total[a : a + LANES, b : b + LANES] + mixed[at_p, at_q] + mixed[at_q, at_p].T
            )


def local_gram(slab):
    rows, second, third = slab.shape
    depth = ROWS
    half = rows // 2
    out = (len(upper_blocks(rows)) * LANES, LANES)
    return pl.pallas_call(
        gram_kernel,
        grid=(second // depth, third // LANES),
        in_specs=[pl.BlockSpec((rows, depth, LANES), lambda j, l: (0, j, l))],
        out_specs=pl.BlockSpec(out, lambda j, l: (0, 0)),
        out_shape=jax.ShapeDtypeStruct(out, f32),
        scratch_shapes=[pltpu.VMEM((rows, depth // 2 * LANES), bf16)] * 4
        + [pltpu.VMEM((half, half), f32)] * 3
        + [pltpu.VMEM((rows, rows), f32)],
        compiler_params=pltpu.CompilerParams(vmem_limit_bytes=50 * MIB),
        name="gram",
    )(slab)


def swap(x, devices, mask):
    return lax.ppermute(x, ("wide", "narrow"), [(i, i ^ mask) for i in range(devices)])


def masks_of(bits):
    return [sum(bit for i, bit in enumerate(bits) if k >> i & 1) for k in range(1 << len(bits))]


def pairwise(terms):
    while len(terms) > 1:
        terms = [a + b for a, b in zip(terms[::2], terms[1::2])]
    return terms[0]


def scatter_sum(x, devices, bits):
    parts = x.reshape(1 << len(bits), -1, x.shape[-1])
    me = lax.axis_index(("wide", "narrow"))
    place = sum((me & bit) // bit << i for i, bit in enumerate(bits))
    terms = [lax.dynamic_index_in_dim(parts, place ^ k, 0, keepdims=False) for k in range(len(parts))]
    return pairwise(terms[:1] + [swap(t, devices, mask) for t, mask in zip(terms[1:], masks_of(bits)[1:])])


def gather(x, devices, bits):
    me = lax.axis_index(("wide", "narrow"))
    parts = [x] + [swap(x, devices, mask) for mask in masks_of(bits)[1:]]
    for i, bit in enumerate(bits):
        parts = [jnp.where(me & bit == 0, parts[k], parts[k ^ 1 << i]) for k in range(len(parts))]
    return jnp.concatenate(parts)


def total(x, wide, narrow):
    devices = wide * narrow
    core = [1]
    plane = [1 << k for k in range(1, narrow.bit_length())]
    line = [narrow << k for k in range(1, wide.bit_length() - 1)]
    x = scatter_sum(x, devices, core)
    x = scatter_sum(x, devices, plane)
    x = pairwise([x] + [swap(x, devices, mask) for mask in masks_of(line)[1:]])
    x = gather(x, devices, plane)
    return gather(x, devices, core)


def row_of(v, j):
    return jnp.broadcast_to(v[j : j + 1, :], v.shape)


def column_of(v, j):
    return jnp.broadcast_to(v[:, j : j + 1], v.shape)


def inverse_factor(inner, exact):
    n = inner.shape[0]
    groups = n // ROWS
    row = lax.broadcasted_iota(jnp.int32, (ROWS, 2 * n), 0)
    unit = lax.broadcasted_iota(jnp.int32, (n, n), 0) == lax.broadcasted_iota(jnp.int32, (n, n), 1)
    both = jnp.concatenate([inner, unit.astype(f32)], axis=1)
    m = [both[ROWS * q : ROWS * (q + 1)] for q in range(groups)]
    out = []
    for p in range(groups):
        column = {(q, j): column_of(m[q], ROWS * p + j) for q in range(p, groups) for j in range(ROWS)}
        pivots = None
        for j in range(ROWS):
            pivot = row_of(column[p, j], j)
            inverse = pltpu.reciprocal(pivot, approx=True)
            if exact:
                inverse = inverse * (2.0 - pivot * inverse)
                inverse = inverse * (2.0 - pivot * inverse)
            pivots = pivot if pivots is None else jnp.where(row >= j, pivot, pivots)
            later = {k: row_of(column[p, k], j) for k in range(j + 1, ROWS)}
            pivot_row = row_of(m[p], j)
            for q in range(p, groups):
                factor = column[q, j] * inverse
                if q == p:
                    factor = jnp.where(row > j, factor, 0.0)
                for k in range(j + 1, ROWS):
                    column[q, k] = column[q, k] - factor * later[k]
                m[q] = m[q] - factor * pivot_row
        scale = lax.rsqrt(pivots)
        if exact:
            scale = scale * (1.5 - 0.5 * pivots * scale * scale)
        out.append(m[p] * scale)
    return jnp.concatenate(out, axis=0)[:, n:]


def iterate_kernel(order_ref, packed_ref, start_ref, slab_ref, basis_ref, *rest):
    *out_refs, high, low, by_group, slab, sems = rest
    blocks, strips, rows, depth, lanes = slab.shape
    copies = [
        pltpu.make_async_copy(
            slab_ref.at[:, pl.ds(s * depth, depth), pl.ds(l * lanes, lanes)], slab.at[l, s], sems.at[l, s]
        )
        for l in range(blocks)
        for s in range(strips)
    ]
    for copy in copies:
        copy.start()

    for k, (p, q) in enumerate(upper_blocks(high.shape[0])):
        at_p, at_q = slice(p * LANES, (p + 1) * LANES), slice(q * LANES, (q + 1) * LANES)
        block = packed_ref[k * LANES : (k + 1) * LANES]
        high[at_p, at_q], low[at_p, at_q] = two(block)
        if p != q:
            high[at_q, at_p], low[at_q, at_p] = two(block.T)

    def times_gram(b):
        return dot_two(b, (high[...], low[...]), NN)

    basis_ref[...] = times_gram(two(start_ref[...]))

    def sweep(_, carry):
        block = two(basis_ref[...])
        product = times_gram(block)
        inverse = inverse_factor(dot_two(block, block, NT), False)
        basis_ref[...] = dot_two(two(inverse), two(product), NN)
        return carry

    lax.fori_loop(0, ITERS - 1, sweep, 0)
    block = basis_ref[...]
    inverse = inverse_factor(dot_full(block, block, NT), True)
    basis_ref[...] = dot_full(inverse, block, NN)

    rank = basis_ref.shape[0]
    size = rank // len(out_refs)
    for g in range(len(out_refs)):
        by_group[g] = basis_ref[g * size : (g + 1) * size]
    basis = jnp.concatenate([by_group[order_ref[g]] for g in range(len(out_refs))], axis=0)
    basis = jnp.concatenate(two(basis), axis=0)
    flat = slab.reshape(blocks * strips * rows * depth, lanes)
    for copy in copies:
        copy.wait()

    def columns(step, carry):
        for j in range(0, depth, 2):
            at = step * rows * depth + j
            pair = [two(flat[pl.ds(at + k, rows, stride=depth), :]) for k in range(2)]
            high_x, low_x = (jnp.concatenate(half, axis=1) for half in zip(*pair))
            by_high = dot(basis, high_x, NN)
            field = by_high[:rank] + (by_high[rank:] + dot(basis[:rank], low_x, NN))
            for k in range(2):
                for g, out_ref in enumerate(out_refs):
                    out_ref[step // strips, step % strips * depth + j + k] = field[
                        g * size : (g + 1) * size, k * lanes : (k + 1) * lanes
                    ]
        return carry

    lax.fori_loop(0, blocks * strips, columns, 0)


def iterate(order, packed, start, tensor_slab):
    rank, n = start.shape
    rows, second, third = tensor_slab.shape
    groups = order.shape[0]
    field = jax.ShapeDtypeStruct((third // LANES, second, rank // groups, LANES), f32)
    vmem = pl.BlockSpec(memory_space=pltpu.VMEM)
    return pl.pallas_call(
        iterate_kernel,
        in_specs=[pl.BlockSpec(memory_space=pltpu.SMEM), vmem, vmem, pl.BlockSpec(memory_space=pl.ANY)],
        out_specs=[vmem] * (1 + groups),
        out_shape=[jax.ShapeDtypeStruct((rank, n), f32)] + [field] * groups,
        scratch_shapes=[pltpu.VMEM((n, n), bf16)] * 2
        + [pltpu.VMEM((groups, rank // groups, n), f32)]
        + [
            pltpu.VMEM((third // LANES, second // DEPTH, rows, DEPTH, LANES), f32),
            pltpu.SemaphoreType.DMA((third // LANES, second // DEPTH)),
        ],
        compiler_params=pltpu.CompilerParams(vmem_limit_bytes=44 * MIB),
        name="iterate",
    )(order, packed, start, tensor_slab)


def exchange(parts, wide, narrow, near):
    def move(mask, part):
        return swap(part, wide * narrow, mask * narrow)

    received = {0: parts[0]}
    early = [*range(wide - 1, near, -1), *range(near - 1, 0, -2)]
    for mask in early:
        received[mask] = move(mask, parts[mask])
    late = [mask for mask in range(near, 0, -1) if mask not in early]
    *arrived, held = lax.optimization_barrier(
        (*[received[mask] for mask in range(near - 1, 0, -2)], [parts[mask] for mask in late])
    )
    received.update(zip(range(near - 1, 0, -2), arrived))
    for mask, part in zip(late, held):
        received[mask] = move(mask, part)
    return [received[mask] for mask in range(near)], [received[mask] for mask in range(near, wide)]


def turn_kernel(tiles_ref, order_ref, *refs):
    refs = refs[-2 - order_ref.shape[0] :]
    *in_refs, out_ref, held = refs
    _, second, rank, lanes = in_refs[0].shape
    step = LANES // second
    at = pl.program_id(1)

    @pl.when(at == 0)
    def _():
        for s, in_ref in enumerate(in_refs):
            held[s // step * step + order_ref[s]] = in_ref[0]

    flat = held.reshape(len(in_refs) * second * rank, lanes)
    flat_out = out_ref.reshape(lanes * rank, LANES)
    first = at * (step * second * rank)
    for r in range(rank):
        rows = flat[pl.ds(first + r, step * second, stride=rank), :]
        flat_out[pl.ds(r, lanes, stride=rank), :] = rows.T


def turn(tiles, order, parts, sources, before=None):
    blocks, second, rank, lanes = parts[0].shape
    part = pl.BlockSpec((1, second, rank, lanes), lambda l, s, tiles, order: (l, 0, 0, 0))
    earlier = [] if before is None else [before]
    return pl.pallas_call(
        turn_kernel,
        grid_spec=pltpu.PrefetchScalarGridSpec(
            num_scalar_prefetch=2,
            grid=(blocks, len(parts) * second // LANES),
            in_specs=[pl.BlockSpec(memory_space=pl.ANY)] * len(earlier) + [part] * len(parts),
            out_specs=pl.BlockSpec((lanes, rank, LANES), lambda l, s, tiles, order: (l, 0, tiles[s])),
            scratch_shapes=[pltpu.VMEM((len(parts), second, rank, lanes), f32)],
        ),
        out_shape=jax.ShapeDtypeStruct((blocks * lanes, rank, sources * second), f32),
        input_output_aliases={2: 0} if earlier else {},
        compiler_params=pltpu.CompilerParams(vmem_limit_bytes=32 * MIB),
        name="turn",
    )(tiles, order, *earlier, *parts)


def shards(wide, narrow, tensor_slab, start_basis):
    near = LANES // tensor_slab.shape[1]
    me = lax.axis_index("wide")
    order = (me ^ jnp.arange(wide)).astype(jnp.int32)
    tiles = (me // near ^ jnp.arange(wide // near)).astype(jnp.int32)
    places = order % near
    packed = total(local_gram(tensor_slab), wide, narrow)
    basis, *parts = iterate(order, packed, start_basis.T, tensor_slab)
    first, rest = exchange(parts, wide, narrow, near)
    field = turn(tiles[:1], places[:near], first, wide)
    return basis.T, turn(tiles[1:], places[near:], rest, wide, field)


def solution(mesh):
    return jax.shard_map(
        functools.partial(shards, mesh.shape["wide"], mesh.shape["narrow"]),
        mesh=mesh,
        in_specs=(P(None, "wide", "narrow"), P()),
        out_specs=(P(), P("narrow", "wide", None)),
        check_vma=False,
    )
```

```python
import functools

import jax
import jax.numpy as jnp
from jax import lax
from jax.experimental import pallas as pl
from jax.experimental.pallas import tpu as pltpu
from jax.sharding import PartitionSpec as P

ITERS = 8
LANES = 128
ROWS = 8
DEPTH = 4
MIB = 2**20
NT = (((1,), (1,)), ((), ()))
NN = (((1,), (0,)), ((), ()))
f32, bf16 = jnp.float32, jnp.bfloat16


def dot(a, b, dims):
    return lax.dot_general(a, b, dims, preferred_element_type=f32)


def dot_full(a, b, dims):
    return lax.dot_general(a, b, dims, precision=lax.Precision.HIGHEST, preferred_element_type=f32)


def two(x):
    high = x.astype(bf16)
    return high, (x - high.astype(f32)).astype(bf16)


def dot_two(a, b, dims):
    (a_high, a_low), (b_high, b_low) = a, b
    return dot(a_high, b_high, dims) + (dot(a_high, b_low, dims) + dot(a_low, b_high, dims))


def upper_blocks(n):
    return [(p, q) for p in range(n // LANES) for q in range(p, n // LANES)]


def split_rows(x_ref, first, count, high, low):
    rows, depth, lanes = x_ref.shape
    flat = x_ref.reshape(rows * depth, lanes)
    for j in range(count):
        a, b = two(flat[pl.ds(first + j, rows, stride=depth), :])
        high[:, j * lanes : (j + 1) * lanes] = a
        low[:, j * lanes : (j + 1) * lanes] = b


def gram_kernel(x_ref, g_ref, high_0, low_0, high_1, low_1, top, cross, bottom, mixed):
    rows, depth, _ = x_ref.shape
    half = rows // 2
    steps = pl.num_programs(0) * pl.num_programs(1)
    step = pl.program_id(0) * pl.num_programs(1) + pl.program_id(1)

    def add(high, low):
        mixed[...] += dot(high[...], low[...], NT)
        top[...] += dot(high[:half], high[:half], NT)
        cross[...] += dot(high[:half], high[half:], NT)
        bottom[...] += dot(high[half:], high[half:], NT)

    @pl.when(step == 0)
    def _():
        for total in (top, cross, bottom, mixed):
            total[...] = jnp.zeros_like(total)
        split_rows(x_ref, 0, depth // 2, high_0, low_0)
        split_rows(x_ref, depth // 2, depth // 2, high_1, low_1)
        add(high_0, low_0)

    @pl.when(step > 0)
    def _():
        add(high_1, low_1)
        split_rows(x_ref, 0, depth // 2, high_0, low_0)
        add(high_0, low_0)
        split_rows(x_ref, depth // 2, depth // 2, high_1, low_1)

    @pl.when(step == steps - 1)
    def _():
        add(high_1, low_1)
        for k, (p, q) in enumerate(upper_blocks(rows)):
            in_half = half // LANES
            total = top if q < in_half else cross if p < in_half else bottom
            a, b = p % in_half * LANES, q % in_half * LANES
            at_p, at_q = slice(p * LANES, (p + 1) * LANES), slice(q * LANES, (q + 1) * LANES)
            g_ref[k * LANES : (k + 1) * LANES] = (
                total[a : a + LANES, b : b + LANES] + mixed[at_p, at_q] + mixed[at_q, at_p].T
            )


def local_gram(slab):
    rows, second, third = slab.shape
    depth = ROWS
    half = rows // 2
    out = (len(upper_blocks(rows)) * LANES, LANES)
    return pl.pallas_call(
        gram_kernel,
        grid=(second // depth, third // LANES),
        in_specs=[pl.BlockSpec((rows, depth, LANES), lambda j, l: (0, j, l))],
        out_specs=pl.BlockSpec(out, lambda j, l: (0, 0)),
        out_shape=jax.ShapeDtypeStruct(out, f32),
        scratch_shapes=[pltpu.VMEM((rows, depth // 2 * LANES), bf16)] * 4
        + [pltpu.VMEM((half, half), f32)] * 3
        + [pltpu.VMEM((rows, rows), f32)],
        compiler_params=pltpu.CompilerParams(vmem_limit_bytes=50 * MIB),
        name="gram",
    )(slab)


def swap(x, devices, mask):
    return lax.ppermute(x, ("wide", "narrow"), [(i, i ^ mask) for i in range(devices)])


def masks_of(bits):
    return [sum(bit for i, bit in enumerate(bits) if k >> i & 1) for k in range(1 << len(bits))]


def pairwise(terms):
    while len(terms) > 1:
        terms = [a + b for a, b in zip(terms[::2], terms[1::2])]
    return terms[0]


def scatter_sum(x, devices, bits):
    parts = x.reshape(1 << len(bits), -1, x.shape[-1])
    me = lax.axis_index(("wide", "narrow"))
    place = sum((me & bit) // bit << i for i, bit in enumerate(bits))
    terms = [lax.dynamic_index_in_dim(parts, place ^ k, 0, keepdims=False) for k in range(len(parts))]
    return pairwise(terms[:1] + [swap(t, devices, mask) for t, mask in zip(terms[1:], masks_of(bits)[1:])])


def gather(x, devices, bits):
    me = lax.axis_index(("wide", "narrow"))
    parts = [x] + [swap(x, devices, mask) for mask in masks_of(bits)[1:]]
    for i, bit in enumerate(bits):
        parts = [jnp.where(me & bit == 0, parts[k], parts[k ^ 1 << i]) for k in range(len(parts))]
    return jnp.concatenate(parts)


def total(x, wide, narrow):
    devices = wide * narrow
    core = [1]
    plane = [1 << k for k in range(1, narrow.bit_length())]
    line = [narrow << k for k in range(1, wide.bit_length() - 1)]
    x = scatter_sum(x, devices, core)
    x = scatter_sum(x, devices, plane)
    x = pairwise([x] + [swap(x, devices, mask) for mask in masks_of(line)[1:]])
    x = gather(x, devices, plane)
    return gather(x, devices, core)


def row_of(v, j):
    return jnp.broadcast_to(v[j : j + 1, :], v.shape)


def column_of(v, j):
    return jnp.take_along_axis(v, jnp.full(v.shape, j, jnp.int32), axis=1, mode="promise_in_bounds")


def inverse_factor(inner, exact):
    n = inner.shape[0]
    groups = n // ROWS
    row = lax.broadcasted_iota(jnp.int32, (ROWS, 2 * n), 0)
    unit = lax.broadcasted_iota(jnp.int32, (n, n), 0) == lax.broadcasted_iota(jnp.int32, (n, n), 1)
    both = jnp.concatenate([inner, unit.astype(f32)], axis=1)
    m = [both[ROWS * q : ROWS * (q + 1)] for q in range(groups)]
    out = []
    for p in range(groups):
        column = {(q, j): column_of(m[q], ROWS * p + j) for q in range(p, groups) for j in range(ROWS)}
        pivots = None
        for j in range(ROWS):
            pivot = row_of(column[p, j], j)
            inverse = pltpu.reciprocal(pivot, approx=True)
            if exact:
                inverse = inverse * (2.0 - pivot * inverse)
                inverse = inverse * (2.0 - pivot * inverse)
            pivots = pivot if pivots is None else jnp.where(row >= j, pivot, pivots)
            later = {k: row_of(column[p, k], j) for k in range(j + 1, ROWS)}
            pivot_row = row_of(m[p], j)
            for q in range(p, groups):
                factor = column[q, j] * inverse
                if q == p:
                    factor = jnp.where(row > j, factor, 0.0)
                for k in range(j + 1, ROWS):
                    column[q, k] = column[q, k] - factor * later[k]
                m[q] = m[q] - factor * pivot_row
        scale = lax.rsqrt(pivots)
        if exact:
            scale = scale * (1.5 - 0.5 * pivots * scale * scale)
        out.append(m[p] * scale)
    return jnp.concatenate(out, axis=0)[:, n:]


def iterate_kernel(packed_ref, start_ref, slab_ref, basis_ref, *rest):
    *out_refs, high, low, by_group, slab, sems = rest
    blocks, strips, rows, depth, lanes = slab.shape
    copies = [
        pltpu.make_async_copy(
            slab_ref.at[:, pl.ds(s * depth, depth), pl.ds(l * lanes, lanes)], slab.at[l, s], sems.at[l, s]
        )
        for l in range(blocks)
        for s in range(strips)
    ]
    for copy in copies:
        copy.start()

    for k, (p, q) in enumerate(upper_blocks(high.shape[0])):
        at_p, at_q = slice(p * LANES, (p + 1) * LANES), slice(q * LANES, (q + 1) * LANES)
        block = packed_ref[k * LANES : (k + 1) * LANES]
        high[at_p, at_q], low[at_p, at_q] = two(block)
        if p != q:
            high[at_q, at_p], low[at_q, at_p] = two(block.T)

    def times_gram(b):
        return dot_two(b, (high[...], low[...]), NN)

    basis_ref[...] = times_gram(two(start_ref[...]))

    def sweep(_, carry):
        block = two(basis_ref[...])
        product = times_gram(block)
        inverse = inverse_factor(dot_two(block, block, NT), False)
        basis_ref[...] = dot_two(two(inverse), two(product), NN)
        return carry

    lax.fori_loop(0, ITERS - 1, sweep, 0)
    block = basis_ref[...]
    inverse = inverse_factor(dot_full(block, block, NT), True)
    basis_ref[...] = dot_full(inverse, block, NN)

    rank = basis_ref.shape[0]
    size = rank // len(out_refs)
    me = lax.axis_index("wide")
    for g in range(len(out_refs)):
        by_group[g] = basis_ref[g * size : (g + 1) * size]
    basis = jnp.concatenate([by_group[me ^ g] for g in range(len(out_refs))], axis=0)
    basis = jnp.concatenate(two(basis), axis=0)
    flat = slab.reshape(blocks * strips * rows * depth, lanes)
    for copy in copies:
        copy.wait()

    def columns(step, carry):
        for j in range(0, 2 * depth, 2):
            strip = step * 2 + j // depth
            at = strip * rows * depth + j % depth
            pair = [two(flat[pl.ds(at + k, rows, stride=depth), :]) for k in range(2)]
            high_x, low_x = (jnp.concatenate(half, axis=1) for half in zip(*pair))
            by_high = dot(basis, high_x, NN)
            field = by_high[:rank] + (by_high[rank:] + dot(basis[:rank], low_x, NN))
            for k in range(2):
                for g, out_ref in enumerate(out_refs):
                    out_ref[step * 2 // strips, step * 2 % strips * depth + j + k] = field[
                        g * size : (g + 1) * size, k * lanes : (k + 1) * lanes
                    ]
        return carry

    lax.fori_loop(0, blocks * strips // 2, columns, 0)


def iterate(packed, start, tensor_slab, groups):
    rank, n = start.shape
    rows, second, third = tensor_slab.shape
    field = jax.ShapeDtypeStruct((third // LANES, second, rank // groups, LANES), f32)
    vmem = pl.BlockSpec(memory_space=pltpu.VMEM)
    return pl.pallas_call(
        iterate_kernel,
        in_specs=[vmem, vmem, pl.BlockSpec(memory_space=pl.ANY)],
        out_specs=[vmem] * (1 + groups),
        out_shape=[jax.ShapeDtypeStruct((rank, n), f32)] + [field] * groups,
        scratch_shapes=[pltpu.VMEM((n, n), bf16)] * 2
        + [pltpu.VMEM((groups, rank // groups, n), f32)]
        + [
            pltpu.VMEM((third // LANES, second // DEPTH, rows, DEPTH, LANES), f32),
            pltpu.SemaphoreType.DMA((third // LANES, second // DEPTH)),
        ],
        compiler_params=pltpu.CompilerParams(vmem_limit_bytes=44 * MIB),
        name="iterate",
    )(packed, start, tensor_slab)


def exchange(parts, wide, narrow, near):
    def move(mask, part):
        return swap(part, wide * narrow, mask * narrow)

    received = {0: parts[0]}
    for mask in [*range(wide - 1, near - 1, -1), *range(1, near, 2)]:
        received[mask] = move(mask, parts[mask])
    late = range(2, near, 2)
    received[1], held = lax.optimization_barrier((received[1], [parts[mask] for mask in late]))
    for mask, part in zip(late, held):
        received[mask] = move(mask, part)
    return [received[mask] for mask in range(wide)]


def turn_kernel(*refs):
    *in_refs, out_ref, held, turned, sems = refs
    sources = len(in_refs)
    _, second, rank, lanes = held.shape
    step = LANES // second
    me = lax.axis_index("wide")
    flat = held.reshape(sources * second * rank, lanes)
    tiles = sources // step
    copies = []
    for block in range(in_refs[0].shape[0]):
        for s, in_ref in enumerate(in_refs):
            held[s // step * step + (me ^ s) % step] = in_ref[block]
        for tile in range(tiles):
            index = block * tiles + tile
            flat_out = turned.at[index].reshape(lanes * rank, LANES)
            for r in range(rank):
                rows = flat[pl.ds(tile * step * second * rank + r, step * second, stride=rank), :]
                flat_out[pl.ds(r, lanes, stride=rank), :] = rows.T
            columns = pl.ds(pl.multiple_of((me // step ^ tile) * LANES, LANES), LANES)
            copy = pltpu.make_async_copy(
                turned.at[index], out_ref.at[pl.ds(block * lanes, lanes), :, columns], sems.at[index]
            )
            copy.start()
            copies.append(copy)
    for copy in copies:
        copy.wait()


def turn(parts):
    blocks, second, rank, lanes = parts[0].shape
    vmem, anywhere = (pl.BlockSpec(memory_space=space) for space in (pltpu.VMEM, pl.ANY))
    pieces = blocks * len(parts) * second // LANES
    return pl.pallas_call(
        turn_kernel,
        in_specs=[vmem] * len(parts),
        out_specs=anywhere,
        out_shape=jax.ShapeDtypeStruct((blocks * lanes, rank, len(parts) * second), f32),
        scratch_shapes=[
            pltpu.VMEM((len(parts), second, rank, lanes), f32),
            pltpu.VMEM((pieces, lanes, rank, LANES), f32),
            pltpu.SemaphoreType.DMA((pieces,)),
        ],
        compiler_params=pltpu.CompilerParams(vmem_limit_bytes=32 * MIB),
        name="turn",
    )(*parts)


def shards(wide, narrow, tensor_slab, start_basis):
    near = LANES // tensor_slab.shape[1]
    packed = total(local_gram(tensor_slab), wide, narrow)
    basis, *parts = iterate(packed, start_basis.T, tensor_slab, wide)
    return basis.T, turn(exchange(parts, wide, narrow, near))


def solution(mesh):
    return jax.shard_map(
        functools.partial(shards, mesh.shape["wide"], mesh.shape["narrow"]),
        mesh=mesh,
        in_specs=(P(None, "wide", "narrow"), P()),
        out_specs=(P(), P("narrow", "wide", None)),
        check_vma=False,
    )
```

```python
import functools

import jax
import jax.numpy as jnp
from jax import lax
from jax.experimental import pallas as pl
from jax.experimental.pallas import tpu as pltpu
from jax.sharding import PartitionSpec as P

ITERS = 8
LANES = 128
ROWS = 8
DEPTH = 4
MIB = 2**20
NT = (((1,), (1,)), ((), ()))
NN = (((1,), (0,)), ((), ()))
f32, bf16 = jnp.float32, jnp.bfloat16


def dot(a, b, dims):
    return lax.dot_general(a, b, dims, preferred_element_type=f32)


def dot_full(a, b, dims):
    return lax.dot_general(a, b, dims, precision=lax.Precision.HIGHEST, preferred_element_type=f32)


def two(x):
    high = x.astype(bf16)
    return high, (x - high.astype(f32)).astype(bf16)


def dot_two(a, b, dims):
    (a_high, a_low), (b_high, b_low) = a, b
    return dot(a_high, b_high, dims) + (dot(a_high, b_low, dims) + dot(a_low, b_high, dims))


def upper_blocks(n):
    return [(p, q) for p in range(n // LANES) for q in range(p, n // LANES)]


def split_rows(x_ref, first, count, high, low):
    rows, depth, lanes = x_ref.shape
    flat = x_ref.reshape(rows * depth, lanes)
    for j in range(count):
        a, b = two(flat[pl.ds(first + j, rows, stride=depth), :])
        high[:, j * lanes : (j + 1) * lanes] = a
        low[:, j * lanes : (j + 1) * lanes] = b


def gram_kernel(x_ref, g_ref, high_0, low_0, high_1, low_1, top, cross, bottom, mixed):
    rows, depth, _ = x_ref.shape
    half = rows // 2
    steps = pl.num_programs(0) * pl.num_programs(1)
    step = pl.program_id(0) * pl.num_programs(1) + pl.program_id(1)

    def add(high, low):
        mixed[...] += dot(high[...], low[...], NT)
        top[...] += dot(high[:half], high[:half], NT)
        cross[...] += dot(high[:half], high[half:], NT)
        bottom[...] += dot(high[half:], high[half:], NT)

    @pl.when(step == 0)
    def _():
        for total in (top, cross, bottom, mixed):
            total[...] = jnp.zeros_like(total)
        split_rows(x_ref, 0, depth // 2, high_0, low_0)
        split_rows(x_ref, depth // 2, depth // 2, high_1, low_1)
        add(high_0, low_0)

    @pl.when(step > 0)
    def _():
        add(high_1, low_1)
        split_rows(x_ref, 0, depth // 2, high_0, low_0)
        add(high_0, low_0)
        split_rows(x_ref, depth // 2, depth // 2, high_1, low_1)

    @pl.when(step == steps - 1)
    def _():
        add(high_1, low_1)
        for k, (p, q) in enumerate(upper_blocks(rows)):
            in_half = half // LANES
            total = top if q < in_half else cross if p < in_half else bottom
            a, b = p % in_half * LANES, q % in_half * LANES
            at_p, at_q = slice(p * LANES, (p + 1) * LANES), slice(q * LANES, (q + 1) * LANES)
            g_ref[k * LANES : (k + 1) * LANES] = (
                total[a : a + LANES, b : b + LANES] + mixed[at_p, at_q] + mixed[at_q, at_p].T
            )


def local_gram(slab):
    rows, second, third = slab.shape
    depth = ROWS
    half = rows // 2
    out = (len(upper_blocks(rows)) * LANES, LANES)
    return pl.pallas_call(
        gram_kernel,
        grid=(second // depth, third // LANES),
        in_specs=[pl.BlockSpec((rows, depth, LANES), lambda j, l: (0, j, l))],
        out_specs=pl.BlockSpec(out, lambda j, l: (0, 0)),
        out_shape=jax.ShapeDtypeStruct(out, f32),
        scratch_shapes=[pltpu.VMEM((rows, depth // 2 * LANES), bf16)] * 4
        + [pltpu.VMEM((half, half), f32)] * 3
        + [pltpu.VMEM((rows, rows), f32)],
        compiler_params=pltpu.CompilerParams(vmem_limit_bytes=50 * MIB),
        name="gram",
    )(slab)


def swap(x, devices, mask):
    return lax.ppermute(x, ("wide", "narrow"), [(i, i ^ mask) for i in range(devices)])


def masks_of(bits):
    return [sum(bit for i, bit in enumerate(bits) if k >> i & 1) for k in range(1 << len(bits))]


def pairwise(terms):
    while len(terms) > 1:
        terms = [a + b for a, b in zip(terms[::2], terms[1::2])]
    return terms[0]


def scatter_sum(x, devices, bits):
    parts = x.reshape(1 << len(bits), -1, x.shape[-1])
    me = lax.axis_index(("wide", "narrow"))
    place = sum((me & bit) // bit << i for i, bit in enumerate(bits))
    terms = [lax.dynamic_index_in_dim(parts, place ^ k, 0, keepdims=False) for k in range(len(parts))]
    return pairwise(terms[:1] + [swap(t, devices, mask) for t, mask in zip(terms[1:], masks_of(bits)[1:])])


def gather(x, devices, bits):
    me = lax.axis_index(("wide", "narrow"))
    parts = [x] + [swap(x, devices, mask) for mask in masks_of(bits)[1:]]
    for i, bit in enumerate(bits):
        parts = [jnp.where(me & bit == 0, parts[k], parts[k ^ 1 << i]) for k in range(len(parts))]
    return jnp.concatenate(parts)


def total(x, wide, narrow):
    devices = wide * narrow
    core = [1]
    plane = [1 << k for k in range(1, narrow.bit_length())]
    line = [narrow << k for k in range(1, wide.bit_length() - 1)]
    x = scatter_sum(x, devices, core)
    x = scatter_sum(x, devices, plane)
    x = pairwise([x] + [swap(x, devices, mask) for mask in masks_of(line)[1:]])
    x = gather(x, devices, plane)
    return gather(x, devices, core)


def row_of(v, j):
    return jnp.broadcast_to(v[j : j + 1, :], v.shape)


def column_of(v, j):
    return jnp.take_along_axis(v, jnp.full(v.shape, j, jnp.int32), axis=1, mode="promise_in_bounds")


def inverse_factor(inner, exact):
    n = inner.shape[0]
    groups = n // ROWS
    row = lax.broadcasted_iota(jnp.int32, (ROWS, 2 * n), 0)
    unit = lax.broadcasted_iota(jnp.int32, (n, n), 0) == lax.broadcasted_iota(jnp.int32, (n, n), 1)
    both = jnp.concatenate([inner, unit.astype(f32)], axis=1)
    m = [both[ROWS * q : ROWS * (q + 1)] for q in range(groups)]
    out = []
    for p in range(groups):
        column = {(q, j): column_of(m[q], ROWS * p + j) for q in range(p, groups) for j in range(ROWS)}
        pivots = None
        for j in range(ROWS):
            pivot = row_of(column[p, j], j)
            inverse = pltpu.reciprocal(pivot, approx=True)
            if exact:
                inverse = inverse * (2.0 - pivot * inverse)
                inverse = inverse * (2.0 - pivot * inverse)
            pivots = pivot if pivots is None else jnp.where(row >= j, pivot, pivots)
            later = {k: row_of(column[p, k], j) for k in range(j + 1, ROWS)}
            pivot_row = row_of(m[p], j)
            for q in range(p, groups):
                factor = column[q, j] * inverse
                if q == p:
                    factor = jnp.where(row > j, factor, 0.0)
                for k in range(j + 1, ROWS):
                    column[q, k] = column[q, k] - factor * later[k]
                m[q] = m[q] - factor * pivot_row
        scale = lax.rsqrt(pivots)
        if exact:
            scale = scale * (1.5 - 0.5 * pivots * scale * scale)
        out.append(m[p] * scale)
    return jnp.concatenate(out, axis=0)[:, n:]


def iterate_kernel(packed_ref, start_ref, slab_ref, basis_ref, *rest):
    *out_refs, high, low, by_group, slab, sems = rest
    blocks, strips, rows, depth, lanes = slab.shape
    copies = [
        pltpu.make_async_copy(
            slab_ref.at[:, pl.ds(s * depth, depth), pl.ds(l * lanes, lanes)], slab.at[l, s], sems.at[l, s]
        )
        for l in range(blocks)
        for s in range(strips)
    ]
    for copy in copies:
        copy.start()

    for k, (p, q) in enumerate(upper_blocks(high.shape[0])):
        at_p, at_q = slice(p * LANES, (p + 1) * LANES), slice(q * LANES, (q + 1) * LANES)
        block = packed_ref[k * LANES : (k + 1) * LANES]
        high[at_p, at_q], low[at_p, at_q] = two(block)
        if p != q:
            high[at_q, at_p], low[at_q, at_p] = two(block.T)

    def times_gram(b):
        return dot_two(b, (high[...], low[...]), NN)

    basis_ref[...] = times_gram(two(start_ref[...]))

    def sweep(_, carry):
        block = two(basis_ref[...])
        inner = dot_two(block, block, NT)
        product = two(times_gram(block))
        inverse = inverse_factor(inner, False)
        basis_ref[...] = dot_two(two(inverse), product, NN)
        return carry

    lax.fori_loop(0, ITERS - 1, sweep, 0)
    block = basis_ref[...]
    inverse = inverse_factor(dot_full(block, block, NT), True)
    basis_ref[...] = dot_full(inverse, block, NN)

    rank = basis_ref.shape[0]
    size = rank // len(out_refs)
    me = lax.axis_index("wide")
    for g in range(len(out_refs)):
        by_group[g] = basis_ref[g * size : (g + 1) * size]
    basis = jnp.concatenate([by_group[me ^ g] for g in range(len(out_refs))], axis=0)
    basis = jnp.concatenate(two(basis), axis=0)
    flat = slab.reshape(blocks * strips * rows * depth, lanes)
    for copy in copies:
        copy.wait()

    def columns(step, carry):
        for j in range(0, 2 * depth, 2):
            strip = step * 2 + j // depth
            at = strip * rows * depth + j % depth
            pair = [two(flat[pl.ds(at + k, rows, stride=depth), :]) for k in range(2)]
            high_x, low_x = (jnp.concatenate(half, axis=1) for half in zip(*pair))
            by_high = dot(basis, high_x, NN)
            field = by_high[:rank] + (by_high[rank:] + dot(basis[:rank], low_x, NN))
            for k in range(2):
                for g, out_ref in enumerate(out_refs):
                    out_ref[step * 2 // strips, step * 2 % strips * depth + j + k] = field[
                        g * size : (g + 1) * size, k * lanes : (k + 1) * lanes
                    ]
        return carry

    lax.fori_loop(0, blocks * strips // 2, columns, 0)


def iterate(packed, start, tensor_slab, groups):
    rank, n = start.shape
    rows, second, third = tensor_slab.shape
    field = jax.ShapeDtypeStruct((third // LANES, second, rank // groups, LANES), f32)
    vmem = pl.BlockSpec(memory_space=pltpu.VMEM)
    return pl.pallas_call(
        iterate_kernel,
        in_specs=[vmem, vmem, pl.BlockSpec(memory_space=pl.ANY)],
        out_specs=[vmem] * (1 + groups),
        out_shape=[jax.ShapeDtypeStruct((rank, n), f32)] + [field] * groups,
        scratch_shapes=[pltpu.VMEM((n, n), bf16)] * 2
        + [pltpu.VMEM((groups, rank // groups, n), f32)]
        + [
            pltpu.VMEM((third // LANES, second // DEPTH, rows, DEPTH, LANES), f32),
            pltpu.SemaphoreType.DMA((third // LANES, second // DEPTH)),
        ],
        compiler_params=pltpu.CompilerParams(vmem_limit_bytes=44 * MIB),
        name="iterate",
    )(packed, start, tensor_slab)


def exchange(parts, wide, narrow, near):
    def move(mask, part):
        return swap(part, wide * narrow, mask * narrow)

    received = {0: parts[0]}
    for mask in [*range(wide - 1, near - 1, -1), *range(1, near, 2)]:
        received[mask] = move(mask, parts[mask])
    late = range(2, near, 2)
    received[1], held = lax.optimization_barrier((received[1], [parts[mask] for mask in late]))
    for mask, part in zip(late, held):
        received[mask] = move(mask, part)
    return [received[mask] for mask in range(wide)]


def turn_kernel(*refs):
    *in_refs, out_ref, held, turned, sems = refs
    sources = len(in_refs)
    _, second, rank, lanes = held.shape
    step = LANES // second
    me = lax.axis_index("wide")
    flat = held.reshape(sources * second * rank, lanes)
    tiles = sources // step
    copies = []
    for block in range(in_refs[0].shape[0]):
        for s, in_ref in enumerate(in_refs):
            held[s // step * step + (me ^ s) % step] = in_ref[block]
        for tile in range(tiles):
            index = block * tiles + tile
            flat_out = turned.at[index].reshape(lanes * rank, LANES)
            for r in range(rank):
                rows = flat[pl.ds(tile * step * second * rank + r, step * second, stride=rank), :]
                flat_out[pl.ds(r, lanes, stride=rank), :] = rows.T
            columns = pl.ds(pl.multiple_of((me // step ^ tile) * LANES, LANES), LANES)
            copy = pltpu.make_async_copy(
                turned.at[index], out_ref.at[pl.ds(block * lanes, lanes), :, columns], sems.at[index]
            )
            copy.start()
            copies.append(copy)
    for copy in copies:
        copy.wait()


def turn(parts):
    blocks, second, rank, lanes = parts[0].shape
    vmem, anywhere = (pl.BlockSpec(memory_space=space) for space in (pltpu.VMEM, pl.ANY))
    pieces = blocks * len(parts) * second // LANES
    return pl.pallas_call(
        turn_kernel,
        in_specs=[vmem] * len(parts),
        out_specs=anywhere,
        out_shape=jax.ShapeDtypeStruct((blocks * lanes, rank, len(parts) * second), f32),
        scratch_shapes=[
            pltpu.VMEM((len(parts), second, rank, lanes), f32),
            pltpu.VMEM((pieces, lanes, rank, LANES), f32),
            pltpu.SemaphoreType.DMA((pieces,)),
        ],
        compiler_params=pltpu.CompilerParams(vmem_limit_bytes=32 * MIB),
        name="turn",
    )(*parts)


def shards(wide, narrow, tensor_slab, start_basis):
    near = LANES // tensor_slab.shape[1]
    packed = total(local_gram(tensor_slab), wide, narrow)
    basis, *parts = iterate(packed, start_basis.T, tensor_slab, wide)
    return basis.T, turn(exchange(parts, wide, narrow, near))


def solution(mesh):
    return jax.shard_map(
        functools.partial(shards, mesh.shape["wide"], mesh.shape["narrow"]),
        mesh=mesh,
        in_specs=(P(None, "wide", "narrow"), P()),
        out_specs=(P(), P("narrow", "wide", None)),
        check_vma=False,
    )
```
